32 devices in a mesh: particle: 4 (over z), slab: 4 (over y, x), half: 2 (over core).
Axes of the slice: x: 2, y: 2, z: 4, core: 2. Of those that a mesh axis runs over, the one named last changes fastest.
Arguments:
- tiles: bfloat16 [2, 256, 16, 4096], P('half', 'particle', 'slab'), may hold values from -1.5 to 1.5
- tile_index: int32 [2, 256, 16], P('half', 'particle', 'slab'), may hold values from 0 to 2047
- pose_bin: int32 [2, 256], P('half', 'particle'), may hold values from 0 to 31
- bin_gain: bfloat16 [2, 32], P('half'), may hold values from 0.25 to 4
- cutoffs: int32 [6], replicated, may hold values from 32 to 128, as said below
Outputs:
- refined: float32 [2, 256, 256, 256], P('half', None, ('particle', 'slab'))
The draws below stay inside these ranges and needn't reach their ends.
Inputs may be any that keep to these rules, and one draw needn't show every extreme that they name: `cutoffs`: the last band's cutoff is 128.
All inputs are finite; a program needn't handle non-finite values.
Results may differ from the reference program's by a relative error of at most 0.0003.
Values sent between devices are 32-bit elements; how exact they have to be, the bound alone decides.
A program may use at most 256 MiB of HBM per device.

```python
import math
import jax
import jax.numpy as jnp
from jax import lax

BOX = 256
BANDS = 6
TILE_ROWS = 8
TOUCH = 4
POSE_BINS = 32
PARTICLES = 64
SLOTS = 2048
N_PARTICLE = 4
N_SLAB = 4


def draw_cutoffs(key, part):
    drawn = jax.random.randint(key, (BANDS,), BOX // 8, BOX // 2 + 1)
    positions = jnp.arange(BANDS)
    return jnp.where(positions == BANDS - 1, BOX // 2, drawn).astype(jnp.int32)


def with_ends(array, key, least, top_value):
    shape = array.shape
    place = [jax.random.randint(jax.random.fold_in(key, axis), (), 0, shape[axis]) for axis in range(len(shape))]
    array = array.at[tuple(place)].set(least)
    longest = shape.index(max(shape))
    place[longest] = (place[longest] + 1) % shape[longest]
    return array.at[tuple(place)].set(top_value)


def block_levels(stream_key, shape, pieces, least, top_value):
    def one(position, parts):
        draws = jax.random.uniform(jax.random.fold_in(jax.random.fold_in(stream_key, 6), position), (parts,), jnp.float32, least / len(pieces), top_value / len(pieces))
        return jnp.repeat(jnp.exp(draws), shape[position] // parts).reshape((-1,) + (1,) * (len(shape) - position - 1))

    gain = one(*pieces[0])
    for cut in pieces[1:]:
        gain = gain * one(*cut)
    return gain


def scatter_about(rng, shape, width, limit, pieces=(), kind=jnp.bfloat16):
    loudness = block_levels(rng, shape, pieces, -0.22, 0.18) if pieces else 1.0
    values = jax.random.normal(rng, shape, jnp.float32) * width * loudness
    return jnp.minimum(jnp.maximum(values, -limit), limit).astype(kind)


def setup_inputs(seed: int = 0) -> dict:
    splits = jax.random.split(jax.random.key(seed), 6)
    tiles = scatter_about(splits[0], (2, PARTICLES * N_PARTICLE, TOUCH * N_SLAB, 2 * TILE_ROWS * BOX), 0.25, 1.5, ((0, 2), (1, 4), (2, 4)))
    tile_index = with_ends(jax.random.randint(splits[1], (2, PARTICLES * N_PARTICLE, TOUCH * N_SLAB), 0, SLOTS), jax.random.fold_in(splits[1], 1), 0, SLOTS - 1).astype(jnp.int32)
    pose_bin = with_ends(jax.random.randint(splits[2], (2, PARTICLES * N_PARTICLE), 0, POSE_BINS), jax.random.fold_in(splits[2], 1), 0, POSE_BINS - 1).astype(jnp.int32)
    bin_gain = jnp.clip(jnp.exp(math.log(4.0) - 2.7725887 * jax.random.uniform(splits[3], (2, POSE_BINS), jnp.float32) ** block_levels(splits[3], (2, POSE_BINS), ((0, 2),), -0.2, 0.2)), 0.25, 4.0).astype(jnp.bfloat16)
    cutoffs = draw_cutoffs(jax.random.fold_in(splits[5], 71), 0)
    return {"tiles": tiles, "tile_index": tile_index, "pose_bin": pose_bin, "bin_gain": bin_gain, "cutoffs": cutoffs}


error_floor = 1.0


def signed_wave(frequency, length):
    return (frequency + length // 2) % length - length // 2


def half_spectrum(half_tiles, half_index, half_bins, half_gain):
    slab_depth = BOX // N_SLAB
    blocks = BOX // TILE_ROWS
    slot_count = slab_depth * blocks
    touched = half_index.shape[1] // N_SLAB
    particle_gain = half_gain.astype(jnp.float32)[half_bins]

    def one_slab(slab_pos):
        part_tiles = lax.dynamic_slice_in_dim(half_tiles, slab_pos * touched, touched, 1).astype(jnp.float32)
        part_slots = lax.dynamic_slice_in_dim(half_index, slab_pos * touched, touched, 1)
        scaled = part_tiles * particle_gain[:, None, None]
        summed = jax.ops.segment_sum(scaled.reshape(-1, scaled.shape[2]), part_slots.reshape(-1), num_segments=slot_count)
        shaped = summed.reshape(slab_depth, blocks, 2, TILE_ROWS, BOX)
        return jnp.transpose(shaped, (2, 0, 1, 3, 4)).reshape(2, slab_depth, BOX, BOX)

    slabs = lax.map(one_slab, jnp.arange(N_SLAB, dtype=jnp.int32))
    return jnp.transpose(slabs, (1, 0, 2, 3, 4)).reshape(2, BOX, BOX, BOX)


def reference(tiles, tile_index, pose_bin, bin_gain, cutoffs):
    grid = jnp.arange(BOX, dtype=jnp.int32)
    signed_all = signed_wave(grid, BOX)
    square = signed_all * signed_all
    radius = square[:, None, None] + square[None, :, None] + square[None, None, :]
    filtered = []
    for half_id in range(2):
        spectrum = half_spectrum(tiles[half_id], tile_index[half_id], pose_bin[half_id], bin_gain[half_id])
        volume = lax.complex(spectrum[0], spectrum[1])

        def one_band(cutoff_now):
            retained = jnp.where(radius <= cutoff_now * cutoff_now, volume, jnp.zeros_like(volume))
            return jnp.real(jnp.fft.ifftn(retained)) * (BOX * BOX)

        filtered.append(lax.map(one_band, cutoffs))
    first, second = filtered
    smoothed = (first - second) ** 2
    for axis_id in (1, 2, 3):
        smoothed = smoothed + jnp.roll(smoothed, 1, axis=axis_id) + jnp.roll(smoothed, -1, axis=axis_id)
    errors = smoothed / 27.0
    weights = 1.0 / (errors + error_floor)
    total = jnp.sum(weights, axis=0)
    outputs = []
    for band_maps in (first, second):
        outputs.append(jnp.sum(weights * band_maps, axis=0) / total)
    return jnp.stack(outputs)
```

```python
import functools
import math

import jax
import jax.numpy as jnp
from jax import lax
from jax.experimental import pallas as pl
from jax.experimental.pallas import tpu as pltpu
from jax.sharding import PartitionSpec as P

BOX = 256
TILE_ROWS = 8
CHUNK_BANDS = 2

error_floor = 1.0
high = lax.Precision.HIGH


def from_partner(array, axis, bit):
    return lax.ppermute(array, axis, [(i, i ^ 1 << bit) for i in range(lax.axis_size(axis))])


def signed_wave(frequency, length):
    return (frequency + length // 2) % length - length // 2


def turn_table(frequency, places, length):
    phase_step = frequency[..., None] * places % length
    angles = phase_step.astype(jnp.float32) * (2.0 * math.pi / length)
    cosine, sine = jnp.cos(angles), jnp.sin(angles)
    from_real = jnp.stack([cosine, sine], axis=-2)
    from_imag = jnp.stack([-sine, cosine], axis=-2)
    return jnp.stack([from_real, from_imag], axis=-3)


def blend_kernel(first, last, step_planes, *refs):
    if first:
        own_ref, other_ref, low_ref, high_ref, *outs = refs
        num_in = den_in = None
    else:
        own_ref, other_ref, low_ref, high_ref, num_in, den_in, *outs = refs
    if last:
        out_ref, padded, smooth, num_ref, den_ref = outs
    else:
        num_ref, den_ref, padded, smooth = outs
    band = pl.program_id(0)
    depth, rows, width = own_ref.shape[1:]

    @pl.when(band == 0)
    def _():
        if first:
            num_ref[...] = jnp.zeros_like(num_ref)
            den_ref[...] = jnp.zeros_like(den_ref)
        else:
            num_ref[...] = num_in[...]
            den_ref[...] = den_in[...]

    def smooth_rows(step, carry):
        here = pl.ds(step * step_planes, step_planes)
        gap = own_ref[0, here] - other_ref[0, here]
        padded[:, 0:1, :] = low_ref[0, here]
        padded[:, 1 : rows + 1, :] = gap * gap
        padded[:, rows + 1 : rows + 2, :] = high_ref[0, here]
        total = (
            padded[:, 0:rows, :] + padded[:, 1 : rows + 1, :] + padded[:, 2 : rows + 2, :]
        )
        total = total + pltpu.roll(total, 1, 2) + pltpu.roll(total, width - 1, 2)
        smooth[pl.ds(step * step_planes + 1, step_planes)] = total
        return carry

    lax.fori_loop(0, depth // step_planes, smooth_rows, 0)
    smooth[0:1] = smooth[depth : depth + 1]
    smooth[depth + 1 : depth + 2] = smooth[1:2]

    def add_band(step, carry):
        start = step * step_planes
        here = pl.ds(start, step_planes)
        total = (
            smooth[here]
            + smooth[pl.ds(start + 1, step_planes)]
            + smooth[pl.ds(start + 2, step_planes)]
        )
        weight = 1.0 / (total * (1.0 / 27.0) + error_floor)
        num_ref[here] += weight * own_ref[0, here]
        den_ref[here] += weight
        return carry

    lax.fori_loop(0, depth // step_planes, add_band, 0)

    if last:

        @pl.when(band == pl.num_programs(0) - 1)
        def _():
            def divide(step, carry):
                here = pl.ds(step * step_planes, step_planes)
                out_ref[here] = num_ref[here] / den_ref[here]
                return carry

            lax.fori_loop(0, depth // step_planes, divide, 0)


def blend(own, other, low, high_rows, sums, last):
    bands, depth, rows, width = own.shape
    first = sums is None
    step_planes = 8
    map_spec = pl.BlockSpec((1, depth, rows, width), lambda b: (b, 0, 0, 0))
    row_spec = pl.BlockSpec((1, depth, 1, width), lambda b: (b, 0, 0, 0))
    whole = pl.BlockSpec((depth, rows, width), lambda b: (0, 0, 0))
    kept = jax.ShapeDtypeStruct((depth, rows, width), jnp.float32)
    scratch = [
        pltpu.VMEM((step_planes, rows + 2, width), jnp.float32),
        pltpu.VMEM((depth + 2, rows, width), jnp.float32),
    ]
    if last:
        scratch += [pltpu.VMEM((depth, rows, width), jnp.float32)] * 2
    cells = bands * depth * rows * width
    return pl.pallas_call(
        functools.partial(blend_kernel, first, last, step_planes),
        grid=(bands,),
        in_specs=[map_spec, map_spec, row_spec, row_spec] + ([] if first else [whole, whole]),
        out_specs=whole if last else [whole, whole],
        out_shape=kept if last else [kept, kept],
        scratch_shapes=scratch,
        compiler_params=pltpu.CompilerParams(vmem_limit_bytes=60 * 1024 * 1024),
        cost_estimate=pl.CostEstimate(
            flops=20 * cells, bytes_accessed=8 * cells + 16 * cells // bands, transcendentals=0
        ),
    )(own, other, low, high_rows, *([] if first else sums))


def on_device(tiles, tile_index, pose_bin, bin_gain, cutoffs):
    slab_count = lax.axis_size("slab")
    group_count = lax.axis_size("particle")
    slab_pos = lax.axis_index("slab")
    group_pos = lax.axis_index("particle")
    slab_depth = BOX // slab_count
    planes = slab_depth + 1
    group_rows = BOX // group_count
    rows_here = group_rows // slab_count
    blocks = BOX // TILE_ROWS
    slot_count = planes * blocks
    half_box = BOX // 2
    touched = tile_index.shape[2]

    entry_slot = tile_index[0].reshape(-1)
    bin_ids = jnp.arange(bin_gain.shape[1], dtype=jnp.int32)
    particle_gain = jnp.sum(
        jnp.where(
            pose_bin[0][:, None] == bin_ids[None, :], bin_gain[0][None, :].astype(jnp.float32), 0.0
        ),
        axis=1,
    )
    entry_gain = jnp.repeat(particle_gain, touched)
    entries = entry_slot.shape[0]
    parts = tiles[0].reshape(entries, 2, TILE_ROWS, BOX).transpose(0, 2, 1, 3).astype(jnp.float32)
    lane = jnp.arange(128, dtype=jnp.int32)
    notes = jnp.where(
        lane[None, :] == 0,
        entry_slot[:, None].astype(jnp.float32),
        jnp.where(lane[None, :] == 1, entry_gain[:, None], 0.0),
    )

    direct = parts[..., :half_box]
    upper = parts[:, :, :, half_box:]
    turn = lax.broadcasted_iota(jnp.int32, (half_box, half_box), 0)
    target = lax.broadcasted_iota(jnp.int32, (half_box, half_box), 1)
    swap = jnp.where((turn + target == half_box) & (target > 0), 1.0, 0.0).astype(jnp.bfloat16)
    mirrored = jnp.einsum(
        "ercx,xk->erck", upper.astype(jnp.bfloat16), swap, preferred_element_type=jnp.float32
    )
    mirrored = mirrored * jnp.array([1.0, -1.0], jnp.float32)[:, None]
    mirrored = jnp.concatenate([mirrored[:, :1], mirrored[:, :0:-1]], axis=1)

    lone = jnp.sum(
        jnp.where(
            (entry_slot == 0) & (slab_pos == 0), entry_gain * parts[:, 0, 0, half_box], 0.0
        )
    )
    lone = lax.psum(lone, ("particle", "slab"))

    width = 2 * TILE_ROWS * half_box
    send_direct = jnp.concatenate([direct.reshape(entries, width), notes], axis=1)
    send_mirror = jnp.concatenate([mirrored.reshape(entries, width), notes], axis=1)
    send_mirror = lax.ppermute(
        send_mirror, "slab", [(i, slab_count - 1 - i) for i in range(slab_count)]
    )
    all_direct = lax.all_gather(send_direct, "particle", axis=0, tiled=True)
    all_mirror = lax.all_gather(send_mirror, "particle", axis=0, tiled=True)
    all_direct, all_mirror = lax.optimization_barrier((all_direct, all_mirror))

    slot_ids = jnp.arange(slot_count, dtype=jnp.int32)
    slot_d = all_direct[:, width].astype(jnp.int32)
    gain_d = all_direct[:, width + 1]
    slot_m = all_mirror[:, width].astype(jnp.int32)
    gain_m = all_mirror[:, width + 1]
    plane_m, block_m = slab_depth - slot_m // blocks, slot_m % blocks
    slot_m0 = plane_m * blocks + (blocks - block_m) % blocks
    slot_m1 = plane_m * blocks + (blocks - 1 - block_m)
    gains = jnp.concatenate([gain_d, gain_m])

    def placing(slots):
        return jnp.where(slot_ids[:, None] == slots[None, :], gains[None, :], 0.0).astype(
            jnp.bfloat16
        )

    values = jnp.concatenate([all_direct[:, :width], all_mirror[:, :width]], axis=0).astype(
        jnp.bfloat16
    )
    row_width = 2 * half_box
    first_rows = jnp.dot(
        placing(jnp.concatenate([slot_d, slot_m0])),
        values[:, :row_width],
        preferred_element_type=jnp.float32,
    )
    other_rows = jnp.dot(
        placing(jnp.concatenate([slot_d, slot_m1])),
        values[:, row_width:],
        preferred_element_type=jnp.float32,
    )
    spectrum = jnp.concatenate([first_rows, other_rows], axis=1).reshape(
        planes, blocks, TILE_ROWS, 2, half_box
    )

    col_freq = jnp.arange(half_box, dtype=jnp.int32)
    positions = jnp.arange(BOX, dtype=jnp.int32)
    row_freq = positions.reshape(blocks, TILE_ROWS)
    plane_freq = slab_pos * slab_depth + jnp.arange(planes, dtype=jnp.int32)
    plane_sq = signed_wave(plane_freq, BOX) ** 2
    row_sq = signed_wave(row_freq, BOX) ** 2
    radius = plane_sq[:, None, None, None] + row_sq[None, :, :, None] + col_freq**2

    row_table = turn_table(
        row_freq, group_pos * group_rows + jnp.arange(group_rows, dtype=jnp.int32), BOX
    )
    row_table = row_table.reshape(blocks, TILE_ROWS, 2, 2, slab_count, rows_here)
    every_plane = (
        jnp.arange(slab_count, dtype=jnp.int32)[:, None] * slab_depth
        + jnp.arange(planes, dtype=jnp.int32)
    )
    plane_table = turn_table(every_plane, positions, BOX)
    col_table = turn_table(col_freq, positions, BOX)[:, :, 0] / BOX
    sign = jnp.where(positions % 2 == 0, 1.0 / BOX, -1.0 / BOX)

    bands = cutoffs.shape[0]
    around = slab_count * group_count
    forward = [(i, (i + 1) % around) for i in range(around)]
    backward = [((i + 1) % around, i) for i in range(around)]
    sums = None
    for start in range(0, bands, CHUNK_BANDS):
        limit = (cutoffs * cutoffs)[start : start + CHUNK_BANDS]
        inside = radius[None] <= limit[:, None, None, None, None]
        masked = jnp.where(inside[:, :, :, :, None, :], spectrum[None], 0.0)
        rows_done = jnp.einsum("bqwrck,wrcdsy->sbdqyk", masked, row_table, precision=high)
        arrived = lax.all_to_all(rows_done, "slab", split_axis=0, concat_axis=0, tiled=True)
        planes_done = jnp.einsum("sbdqyk,sqdez->bzyek", arrived, plane_table, precision=high)
        filtered = jnp.einsum("bzyek,kex->bzyx", planes_done, col_table, precision=high)
        extra = jnp.where(limit >= half_box * half_box, lone, 0.0)
        filtered = filtered + extra[:, None, None, None] * sign
        other = from_partner(filtered, "half", 0)
        head = (filtered[:, :, :1] - other[:, :, :1]) ** 2
        tail = (filtered[:, :, -1:] - other[:, :, -1:]) ** 2
        low = lax.ppermute(tail, ("particle", "slab"), forward)
        high_rows = lax.ppermute(head, ("particle", "slab"), backward)
        sums = blend(filtered, other, low, high_rows, sums, start + CHUNK_BANDS >= bands)
    return sums[None]


def solution(mesh):
    placed = (
        P("half", "particle", "slab", None),
        P("half", "particle", "slab"),
        P("half", "particle"),
        P("half", None),
        P(),
    )
    return jax.shard_map(
        on_device,
        mesh=mesh,
        in_specs=placed,
        out_specs=P("half", None, ("particle", "slab"), None),
        check_vma=False,
    )
```

```python
import functools
import math

import jax
import jax.numpy as jnp
from jax import lax
from jax.experimental import pallas as pl
from jax.experimental.pallas import tpu as pltpu
from jax.sharding import PartitionSpec as P

BOX = 256
TILE_ROWS = 8
CHUNK_BANDS = 2
COL_PARTS = 2

error_floor = 1.0
high = lax.Precision.HIGH


def from_partner(array, axis, bit):
    return lax.ppermute(array, axis, [(i, i ^ 1 << bit) for i in range(lax.axis_size(axis))])


def signed_wave(frequency, length):
    return (frequency + length // 2) % length - length // 2


def turn_table(frequency, places, length):
    phase_step = frequency[..., None] * places % length
    angles = phase_step.astype(jnp.float32) * (2.0 * math.pi / length)
    cosine, sine = jnp.cos(angles), jnp.sin(angles)
    from_real = jnp.stack([cosine, sine], axis=-2)
    from_imag = jnp.stack([-sine, cosine], axis=-2)
    return jnp.stack([from_real, from_imag], axis=-3)


def blend_kernel(first, last, step_planes, *refs):
    if first:
        own_ref, other_ref, low_ref, high_ref, *outs = refs
        num_in = den_in = None
    else:
        own_ref, other_ref, low_ref, high_ref, num_in, den_in, *outs = refs
    if last:
        out_ref, padded, smooth, num_ref, den_ref = outs
    else:
        num_ref, den_ref, padded, smooth = outs
    band = pl.program_id(0)
    depth, rows, width = own_ref.shape

    @pl.when(band == 0)
    def _():
        if first:
            num_ref[...] = jnp.zeros_like(num_ref)
            den_ref[...] = jnp.zeros_like(den_ref)
        else:
            num_ref[...] = num_in[...]
            den_ref[...] = den_in[...]

    def smooth_rows(step, carry):
        here = pl.ds(step * step_planes, step_planes)
        gap = own_ref[here] - other_ref[here]
        padded[:, 0:1, :] = low_ref[here]
        padded[:, 1 : rows + 1, :] = gap * gap
        padded[:, rows + 1 : rows + 2, :] = high_ref[here]
        total = (
            padded[:, 0:rows, :] + padded[:, 1 : rows + 1, :] + padded[:, 2 : rows + 2, :]
        )
        total = total + pltpu.roll(total, 1, 2) + pltpu.roll(total, width - 1, 2)
        smooth[pl.ds(step * step_planes + 1, step_planes)] = total
        return carry

    lax.fori_loop(0, depth // step_planes, smooth_rows, 0)
    smooth[0:1] = smooth[depth : depth + 1]
    smooth[depth + 1 : depth + 2] = smooth[1:2]

    def add_band(step, carry):
        start = step * step_planes
        here = pl.ds(start, step_planes)
        total = (
            smooth[here]
            + smooth[pl.ds(start + 1, step_planes)]
            + smooth[pl.ds(start + 2, step_planes)]
        )
        weight = 1.0 / (total * (1.0 / 27.0) + error_floor)
        num_ref[here] += weight * own_ref[here]
        den_ref[here] += weight
        return carry

    lax.fori_loop(0, depth // step_planes, add_band, 0)

    if last:

        @pl.when(band == pl.num_programs(0) - 1)
        def _():
            def divide(step, carry):
                here = pl.ds(step * step_planes, step_planes)
                out_ref[here] = num_ref[here] / den_ref[here]
                return carry

            lax.fori_loop(0, depth // step_planes, divide, 0)


def blend(own, other, low, high_rows, sums, bands, last):
    depth, rows, width = own.shape
    width = width // bands
    first = sums is None
    step_planes = 8
    map_spec = pl.BlockSpec((depth, rows, width), lambda b: (0, 0, b))
    row_spec = pl.BlockSpec((depth, 1, width), lambda b: (0, 0, b))
    whole = pl.BlockSpec((depth, rows, width), lambda b: (0, 0, 0))
    kept = jax.ShapeDtypeStruct((depth, rows, width), jnp.float32)
    scratch = [
        pltpu.VMEM((step_planes, rows + 2, width), jnp.float32),
        pltpu.VMEM((depth + 2, rows, width), jnp.float32),
    ]
    if last:
        scratch += [pltpu.VMEM((depth, rows, width), jnp.float32)] * 2
    cells = bands * depth * rows * width
    return pl.pallas_call(
        functools.partial(blend_kernel, first, last, step_planes),
        grid=(bands,),
        in_specs=[map_spec, map_spec, row_spec, row_spec] + ([] if first else [whole, whole]),
        out_specs=whole if last else [whole, whole],
        out_shape=kept if last else [kept, kept],
        scratch_shapes=scratch,
        compiler_params=pltpu.CompilerParams(vmem_limit_bytes=60 * 1024 * 1024),
        cost_estimate=pl.CostEstimate(
            flops=20 * cells, bytes_accessed=8 * cells + 16 * cells // bands, transcendentals=0
        ),
    )(own, other, low, high_rows, *([] if first else sums))


def on_device(tiles, tile_index, pose_bin, bin_gain, cutoffs):
    slab_count = lax.axis_size("slab")
    group_count = lax.axis_size("particle")
    slab_pos = lax.axis_index("slab")
    group_pos = lax.axis_index("particle")
    slab_depth = BOX // slab_count
    planes = slab_depth + 1
    group_rows = BOX // group_count
    rows_here = group_rows // slab_count
    blocks = BOX // TILE_ROWS
    slot_count = planes * blocks
    half_box = BOX // 2
    touched = tile_index.shape[2]

    entry_slot = tile_index[0].reshape(-1)
    bin_ids = jnp.arange(bin_gain.shape[1], dtype=jnp.int32)
    particle_gain = jnp.sum(
        jnp.where(
            pose_bin[0][:, None] == bin_ids[None, :], bin_gain[0][None, :].astype(jnp.float32), 0.0
        ),
        axis=1,
    )
    entry_gain = jnp.repeat(particle_gain, touched)
    entries = entry_slot.shape[0]
    parts = tiles[0].reshape(entries, 2, TILE_ROWS, BOX).transpose(0, 2, 1, 3).astype(jnp.float32)
    lane = jnp.arange(128, dtype=jnp.int32)
    notes = jnp.where(
        lane[None, :] == 0,
        entry_slot[:, None].astype(jnp.float32),
        jnp.where(lane[None, :] == 1, entry_gain[:, None], 0.0),
    )

    direct = parts[..., :half_box]
    upper = parts[:, :, :, half_box:]
    turn = lax.broadcasted_iota(jnp.int32, (half_box, half_box), 0)
    target = lax.broadcasted_iota(jnp.int32, (half_box, half_box), 1)
    swap = jnp.where((turn + target) % half_box == 0, 1.0, 0.0).astype(jnp.bfloat16)
    mirrored = jnp.einsum(
        "ercx,xk->erck", upper.astype(jnp.bfloat16), swap, preferred_element_type=jnp.float32
    )
    col_freq = jnp.arange(half_box, dtype=jnp.int32)
    tile_rows = jnp.arange(TILE_ROWS, dtype=jnp.int32)
    is_lone = (entry_slot == 0) & (slab_pos == 0)
    is_first = (tile_rows[:, None] == 0) & (jnp.arange(2, dtype=jnp.int32) == 0)
    keep = (col_freq > 0) | (is_lone[:, None, None, None] & is_first[None, :, :, None])
    mirrored = jnp.where(keep, mirrored, 0.0) * jnp.array([1.0, -1.0], jnp.float32)[:, None]
    mirrored = jnp.concatenate([mirrored[:, :1], mirrored[:, :0:-1]], axis=1)

    span = half_box // COL_PARTS
    width = 2 * TILE_ROWS * span
    flip = [(i, slab_count - 1 - i) for i in range(slab_count)]

    def columns(array, part):
        cut = array[..., part * span : (part + 1) * span].reshape(entries, width)
        return cut * 2.0

    def gather(array):
        return lax.all_gather(array, "particle", axis=0, tiled=True)

    sent_direct = jnp.concatenate([columns(direct, 0), notes], axis=1)
    sent_mirror = lax.ppermute(
        jnp.concatenate([columns(mirrored, 0), notes], axis=1), "slab", flip
    )
    late_mirror = lax.ppermute(
        jnp.concatenate([columns(mirrored, part) for part in range(1, COL_PARTS)], axis=1),
        "slab",
        flip,
    )
    all_direct = gather(sent_direct)
    sent_mirror, all_direct = lax.optimization_barrier((sent_mirror, all_direct))
    all_mirror = gather(sent_mirror)
    gathered = [(all_direct[:, :width], all_mirror[:, :width])]
    for part in range(1, COL_PARTS):
        late = jnp.concatenate(
            [columns(direct, part), late_mirror[:, (part - 1) * width : part * width]], axis=1
        )
        late, all_mirror = lax.optimization_barrier((late, all_mirror))
        late = lax.optimization_barrier(gather(late))
        gathered.append((late[:, :width], late[:, width:]))

    slot_ids = jnp.arange(slot_count, dtype=jnp.int32)
    slot_d = all_direct[:, width].astype(jnp.int32)
    gain_d = all_direct[:, width + 1]
    slot_m = all_mirror[:, width].astype(jnp.int32)
    gain_m = all_mirror[:, width + 1]
    plane_m, block_m = slab_depth - slot_m // blocks, slot_m % blocks
    slot_m0 = plane_m * blocks + (blocks - block_m) % blocks
    slot_m1 = plane_m * blocks + (blocks - 1 - block_m)
    gains = jnp.concatenate([gain_d, gain_m])

    def placing(slots):
        return jnp.where(slot_ids[:, None] == slots[None, :], gains[None, :], 0.0).astype(
            jnp.bfloat16
        )

    place_first = placing(jnp.concatenate([slot_d, slot_m0]))
    place_other = placing(jnp.concatenate([slot_d, slot_m1]))

    positions = jnp.arange(BOX, dtype=jnp.int32)
    row_freq = positions.reshape(blocks, TILE_ROWS).T
    plane_freq = slab_pos * slab_depth + jnp.arange(planes, dtype=jnp.int32)
    plane_sq = signed_wave(plane_freq, BOX) ** 2
    row_sq = signed_wave(row_freq, BOX) ** 2
    row_table = turn_table(
        row_freq, group_pos * group_rows + jnp.arange(group_rows, dtype=jnp.int32), BOX
    )
    row_table = row_table.reshape(TILE_ROWS, blocks, 2, 2, slab_count, rows_here)
    every_plane = (
        jnp.arange(slab_count, dtype=jnp.int32)[:, None] * slab_depth
        + jnp.arange(planes, dtype=jnp.int32)
    )
    plane_table = turn_table(every_plane, positions, BOX)
    col_table = turn_table(col_freq, positions, BOX)[:, :, 0] / BOX
    same_band = jnp.eye(CHUNK_BANDS, dtype=jnp.float32)
    swing = jnp.where(positions % 2 == 0, 0.0, -2.0 / BOX)

    bands = cutoffs.shape[0]
    starts = range(0, bands, CHUNK_BANDS)
    around = slab_count * group_count
    forward = [(i, (i + 1) % around) for i in range(around)]
    backward = [((i + 1) % around, i) for i in range(around)]
    maps = {}
    sums = None
    before = []
    for part in range(COL_PARTS):
        values = (jnp.concatenate(gathered[part], axis=0) * 0.5).astype(jnp.bfloat16)
        values = values.reshape(-1, TILE_ROWS, 2, 1, span)
        values = jnp.broadcast_to(values, values.shape[:3] + (CHUNK_BANDS, span))
        values = values.reshape(-1, TILE_ROWS, 2, CHUNK_BANDS * span)
        first_rows = jnp.einsum(
            "te,erck->rctk", place_first, values[:, :1], preferred_element_type=jnp.float32
        )
        other_rows = jnp.einsum(
            "te,erck->rctk", place_other, values[:, 1:], preferred_element_type=jnp.float32
        )
        spectrum = jnp.concatenate([first_rows, other_rows], axis=0).reshape(
            TILE_ROWS, 2, planes, blocks, CHUNK_BANDS * span
        )
        cols = col_freq[part * span : (part + 1) * span]
        lanes = jnp.tile(cols, CHUNK_BANDS)
        radius = plane_sq[:, None, None] + row_sq[:, None, :, None] + lanes**2
        lone_place = (slab_pos == slab_count - 1) & (
            (jnp.arange(planes) == slab_depth)[:, None, None] & (lanes == 0)
        )
        radius = jnp.where(lone_place, half_box * half_box, radius)
        part_table = jnp.einsum(
            "kex,bf->ebkfx", col_table[part * span : (part + 1) * span], same_band, precision=lax.Precision.HIGHEST
        )
        part_table = part_table.reshape(2 * CHUNK_BANDS * span, CHUNK_BANDS * BOX)
        for start in starts:
            limit = (cutoffs * cutoffs)[start : start + CHUNK_BANDS]
            inside = radius <= jnp.repeat(limit, span)
            masked = jnp.where(inside[:, None], spectrum, 0.0)
            rows_done = jnp.einsum("rcqwl,rwcdsy->sdqyl", masked, row_table, precision=high)
            if len(before) > 1:
                rows_done, _ = lax.optimization_barrier((rows_done, before[-2]))
            arrived = lax.all_to_all(rows_done, "slab", split_axis=0, concat_axis=0, tiled=True)
            if sums is not None:
                arrived, sums = lax.optimization_barrier((arrived, sums))
            planes_done = jnp.einsum("sdqyl,sqdez->zyel", arrived, plane_table, precision=high)
            planes_done = planes_done.reshape(BOX, rows_here, 2 * CHUNK_BANDS * span)
            filtered = jnp.einsum("zyl,lx->zyx", planes_done, part_table, precision=high)
            if part == 0:
                lone = arrived[slab_count - 1, 0, slab_depth, 0].reshape(CHUNK_BANDS, span)[:, 0]
                filtered = filtered + (lone[:, None] * swing).reshape(-1)
            else:
                filtered = filtered + maps[start]
            maps[start] = filtered
            if part < COL_PARTS - 1:
                before.append(filtered)
                continue
            other = from_partner(filtered, "half", 0)
            head = (filtered[:, :1] - other[:, :1]) ** 2
            tail = (filtered[:, -1:] - other[:, -1:]) ** 2
            low = lax.ppermute(tail, ("particle", "slab"), forward)
            high_rows = lax.ppermute(head, ("particle", "slab"), backward)
            sums = blend(
                filtered, other, low, high_rows, sums, CHUNK_BANDS, start + CHUNK_BANDS >= bands
            )
            before.append(filtered)
    return sums[None]


def solution(mesh):
    placed = (
        P("half", "particle", "slab", None),
        P("half", "particle", "slab"),
        P("half", "particle"),
        P("half", None),
        P(),
    )
    return jax.shard_map(
        on_device,
        mesh=mesh,
        in_specs=placed,
        out_specs=P("half", None, ("particle", "slab"), None),
        check_vma=False,
    )
```

```python
import functools
import math

import jax
import jax.numpy as jnp
from jax import lax
from jax.experimental import pallas as pl
from jax.experimental.pallas import tpu as pltpu
from jax.sharding import PartitionSpec as P

BOX = 256
TILE_ROWS = 8
CHUNK_BANDS = 2
COL_PARTS = 2

error_floor = 1.0
high = lax.Precision.HIGH


def from_partner(array, axis, bit):
    return lax.ppermute(array, axis, [(i, i ^ 1 << bit) for i in range(lax.axis_size(axis))])


def signed_wave(frequency, length):
    return (frequency + length // 2) % length - length // 2


def turn_table(frequency, places, length):
    phase_step = frequency[..., None] * places % length
    angles = phase_step.astype(jnp.float32) * (2.0 * math.pi / length)
    cosine, sine = jnp.cos(angles), jnp.sin(angles)
    from_real = jnp.stack([cosine, sine], axis=-2)
    from_imag = jnp.stack([-sine, cosine], axis=-2)
    return jnp.stack([from_real, from_imag], axis=-3)


def blend_kernel(first, last, step_planes, *refs):
    if first:
        own_ref, other_ref, low_ref, high_ref, *outs = refs
        num_in = den_in = None
    else:
        own_ref, other_ref, low_ref, high_ref, num_in, den_in, *outs = refs
    if last:
        out_ref, padded, smooth, num_ref, den_ref = outs
    else:
        num_ref, den_ref, padded, smooth = outs
    band = pl.program_id(0)
    depth, rows, width = own_ref.shape

    @pl.when(band == 0)
    def _():
        if first:
            num_ref[...] = jnp.zeros_like(num_ref)
            den_ref[...] = jnp.zeros_like(den_ref)
        else:
            num_ref[...] = num_in[...]
            den_ref[...] = den_in[...]

    def smooth_rows(step, carry):
        here = pl.ds(step * step_planes, step_planes)
        gap = own_ref[here] - other_ref[here]
        padded[:, 0:1, :] = low_ref[here]
        padded[:, 1 : rows + 1, :] = gap * gap
        padded[:, rows + 1 : rows + 2, :] = high_ref[here]
        total = (
            padded[:, 0:rows, :] + padded[:, 1 : rows + 1, :] + padded[:, 2 : rows + 2, :]
        )
        total = total + pltpu.roll(total, 1, 2) + pltpu.roll(total, width - 1, 2)
        smooth[pl.ds(step * step_planes + 1, step_planes)] = total
        return carry

    lax.fori_loop(0, depth // step_planes, smooth_rows, 0)
    smooth[0:1] = smooth[depth : depth + 1]
    smooth[depth + 1 : depth + 2] = smooth[1:2]

    def add_band(step, carry):
        start = step * step_planes
        here = pl.ds(start, step_planes)
        total = (
            smooth[here]
            + smooth[pl.ds(start + 1, step_planes)]
            + smooth[pl.ds(start + 2, step_planes)]
        )
        weight = 1.0 / (total * (1.0 / 27.0) + error_floor)
        num_ref[here] += weight * own_ref[here]
        den_ref[here] += weight
        return carry

    lax.fori_loop(0, depth // step_planes, add_band, 0)

    if last:

        @pl.when(band == pl.num_programs(0) - 1)
        def _():
            def divide(step, carry):
                here = pl.ds(step * step_planes, step_planes)
                out_ref[here] = num_ref[here] / den_ref[here]
                return carry

            lax.fori_loop(0, depth // step_planes, divide, 0)


def blend(own, other, low, high_rows, sums, bands, last):
    depth, rows, width = own.shape
    width = width // bands
    first = sums is None
    step_planes = 8
    map_spec = pl.BlockSpec((depth, rows, width), lambda b: (0, 0, b))
    row_spec = pl.BlockSpec((depth, 1, width), lambda b: (0, 0, b))
    whole = pl.BlockSpec((depth, rows, width), lambda b: (0, 0, 0))
    kept = jax.ShapeDtypeStruct((depth, rows, width), jnp.float32)
    scratch = [
        pltpu.VMEM((step_planes, rows + 2, width), jnp.float32),
        pltpu.VMEM((depth + 2, rows, width), jnp.float32),
    ]
    if last:
        scratch += [pltpu.VMEM((depth, rows, width), jnp.float32)] * 2
    cells = bands * depth * rows * width
    return pl.pallas_call(
        functools.partial(blend_kernel, first, last, step_planes),
        grid=(bands,),
        in_specs=[map_spec, map_spec, row_spec, row_spec] + ([] if first else [whole, whole]),
        out_specs=whole if last else [whole, whole],
        out_shape=kept if last else [kept, kept],
        scratch_shapes=scratch,
        compiler_params=pltpu.CompilerParams(vmem_limit_bytes=60 * 1024 * 1024),
        cost_estimate=pl.CostEstimate(
            flops=20 * cells, bytes_accessed=8 * cells + 16 * cells // bands, transcendentals=0
        ),
    )(own, other, low, high_rows, *([] if first else sums))


def on_device(tiles, tile_index, pose_bin, bin_gain, cutoffs):
    slab_count = lax.axis_size("slab")
    group_count = lax.axis_size("particle")
    slab_pos = lax.axis_index("slab")
    group_pos = lax.axis_index("particle")
    slab_depth = BOX // slab_count
    planes = slab_depth + 1
    group_rows = BOX // group_count
    rows_here = group_rows // slab_count
    blocks = BOX // TILE_ROWS
    slot_count = planes * blocks
    half_box = BOX // 2
    touched = tile_index.shape[2]

    entry_slot = tile_index[0].reshape(-1)
    bin_ids = jnp.arange(bin_gain.shape[1], dtype=jnp.int32)
    particle_gain = jnp.sum(
        jnp.where(
            pose_bin[0][:, None] == bin_ids[None, :], bin_gain[0][None, :].astype(jnp.float32), 0.0
        ),
        axis=1,
    )
    entry_gain = jnp.repeat(particle_gain, touched)
    entries = entry_slot.shape[0]
    parts = tiles[0].reshape(entries, 2, TILE_ROWS, BOX).transpose(0, 2, 1, 3).astype(jnp.float32)
    lane = jnp.arange(128, dtype=jnp.int32)
    notes = jnp.where(
        lane[None, :] == 0,
        entry_slot[:, None].astype(jnp.float32),
        jnp.where(lane[None, :] == 1, entry_gain[:, None], 0.0),
    )

    direct = parts[..., :half_box]
    upper = parts[:, :, :, half_box:]
    turn = lax.broadcasted_iota(jnp.int32, (half_box, half_box), 0)
    target = lax.broadcasted_iota(jnp.int32, (half_box, half_box), 1)
    swap = jnp.where((turn + target) % half_box == 0, 1.0, 0.0).astype(jnp.bfloat16)
    mirrored = jnp.einsum(
        "ercx,xk->erck", upper.astype(jnp.bfloat16), swap, preferred_element_type=jnp.float32
    )
    col_freq = jnp.arange(half_box, dtype=jnp.int32)
    tile_rows = jnp.arange(TILE_ROWS, dtype=jnp.int32)
    is_lone = (entry_slot == 0) & (slab_pos == 0)
    is_first = (tile_rows[:, None] == 0) & (jnp.arange(2, dtype=jnp.int32) == 0)
    keep = (col_freq > 0) | (is_lone[:, None, None, None] & is_first[None, :, :, None])
    mirrored = jnp.where(keep, mirrored, 0.0) * jnp.array([1.0, -1.0], jnp.float32)[:, None]
    mirrored = jnp.concatenate([mirrored[:, :1], mirrored[:, :0:-1]], axis=1)

    span = half_box // COL_PARTS
    width = 2 * TILE_ROWS * span
    flip = [(i, slab_count - 1 - i) for i in range(slab_count)]

    def columns(array, part):
        cut = array[..., part * span : (part + 1) * span].reshape(entries, width)
        return cut * 2.0

    def gather(array):
        return lax.all_gather(array, "particle", axis=0, tiled=True)

    sent_direct = jnp.concatenate([columns(direct, 0), notes], axis=1)
    sent_mirror = lax.ppermute(
        jnp.concatenate([columns(mirrored, 0), notes], axis=1), "slab", flip
    )
    late_mirror = lax.ppermute(
        jnp.concatenate([columns(mirrored, part) for part in range(1, COL_PARTS)], axis=1),
        "slab",
        flip,
    )
    all_direct = gather(sent_direct)
    sent_mirror, all_direct = lax.optimization_barrier((sent_mirror, all_direct))
    all_mirror = gather(sent_mirror)
    gathered = [(all_direct[:, :width], all_mirror[:, :width])]
    for part in range(1, COL_PARTS):
        late = jnp.concatenate(
            [columns(direct, part), late_mirror[:, (part - 1) * width : part * width]], axis=1
        )
        late, all_mirror = lax.optimization_barrier((late, all_mirror))
        late = lax.optimization_barrier(gather(late))
        gathered.append((late[:, :width], late[:, width:]))

    slot_ids = jnp.arange(slot_count, dtype=jnp.int32)
    slot_d = all_direct[:, width].astype(jnp.int32)
    gain_d = all_direct[:, width + 1]
    slot_m = all_mirror[:, width].astype(jnp.int32)
    gain_m = all_mirror[:, width + 1]
    plane_m, block_m = slab_depth - slot_m // blocks, slot_m % blocks
    slot_m0 = plane_m * blocks + (blocks - block_m) % blocks
    slot_m1 = plane_m * blocks + (blocks - 1 - block_m)
    gains = jnp.concatenate([gain_d, gain_m])

    def placing(slots):
        return jnp.where(slot_ids[:, None] == slots[None, :], gains[None, :], 0.0).astype(
            jnp.bfloat16
        )

    place_first = placing(jnp.concatenate([slot_d, slot_m0]))
    place_other = placing(jnp.concatenate([slot_d, slot_m1]))

    positions = jnp.arange(BOX, dtype=jnp.int32)
    row_freq = positions.reshape(blocks, TILE_ROWS).T
    plane_freq = slab_pos * slab_depth + jnp.arange(planes, dtype=jnp.int32)
    plane_sq = signed_wave(plane_freq, BOX) ** 2
    row_sq = signed_wave(row_freq, BOX) ** 2
    row_table = turn_table(
        row_freq, group_pos * group_rows + jnp.arange(group_rows, dtype=jnp.int32), BOX
    )
    row_table = row_table.reshape(TILE_ROWS, blocks, 2, 2, slab_count, rows_here)
    every_plane = (
        jnp.arange(slab_count, dtype=jnp.int32)[:, None] * slab_depth
        + jnp.arange(planes, dtype=jnp.int32)
    )
    plane_table = turn_table(every_plane, positions, BOX)
    col_table = turn_table(col_freq, positions, BOX)[:, :, 0] / BOX
    same_band = jnp.eye(CHUNK_BANDS, dtype=jnp.float32)
    swing = jnp.where(positions % 2 == 0, 0.0, -2.0 / BOX)

    bands = cutoffs.shape[0]
    starts = range(0, bands, CHUNK_BANDS)
    around = slab_count * group_count
    forward = [(i, (i + 1) % around) for i in range(around)]
    backward = [((i + 1) % around, i) for i in range(around)]
    maps = {}
    sums = None
    for part in range(COL_PARTS):
        values = (jnp.concatenate(gathered[part], axis=0) * 0.5).astype(jnp.bfloat16)
        values = values.reshape(-1, TILE_ROWS, 2, 1, span)
        values = jnp.broadcast_to(values, values.shape[:3] + (CHUNK_BANDS, span))
        values = values.reshape(-1, TILE_ROWS, 2, CHUNK_BANDS * span)
        first_rows = jnp.einsum(
            "te,erck->rctk", place_first, values[:, :1], preferred_element_type=jnp.float32
        )
        other_rows = jnp.einsum(
            "te,erck->rctk", place_other, values[:, 1:], preferred_element_type=jnp.float32
        )
        spectrum = jnp.concatenate([first_rows, other_rows], axis=0).reshape(
            TILE_ROWS, 2, planes, blocks, CHUNK_BANDS * span
        )
        cols = col_freq[part * span : (part + 1) * span]
        lanes = jnp.tile(cols, CHUNK_BANDS)
        radius = plane_sq[:, None, None] + row_sq[:, None, :, None] + lanes**2
        lone_place = (slab_pos == slab_count - 1) & (
            (jnp.arange(planes) == slab_depth)[:, None, None] & (lanes == 0)
        )
        radius = jnp.where(lone_place, half_box * half_box, radius)
        part_table = jnp.einsum(
            "kex,bf->ebkfx", col_table[part * span : (part + 1) * span], same_band, precision=lax.Precision.HIGHEST
        )
        part_table = part_table.reshape(2 * CHUNK_BANDS * span, CHUNK_BANDS * BOX)
        for start in starts:
            limit = (cutoffs * cutoffs)[start : start + CHUNK_BANDS]
            inside = radius <= jnp.repeat(limit, span)
            masked = jnp.where(inside[:, None], spectrum, 0.0)
            rows_done = jnp.einsum("rcqwl,rwcdsy->sdqyl", masked, row_table, precision=high)
            arrived = lax.all_to_all(rows_done, "slab", split_axis=0, concat_axis=0, tiled=True)
            planes_done = jnp.einsum("sdqyl,sqdez->zyel", arrived, plane_table, precision=high)
            planes_done = planes_done.reshape(BOX, rows_here, 2 * CHUNK_BANDS * span)
            filtered = jnp.einsum("zyl,lx->zyx", planes_done, part_table, precision=high)
            if part == 0:
                lone = arrived[slab_count - 1, 0, slab_depth, 0].reshape(CHUNK_BANDS, span)[:, 0]
                filtered = filtered + (lone[:, None] * swing).reshape(-1)
            else:
                filtered = filtered + maps[start]
            maps[start] = filtered
            if part < COL_PARTS - 1:
                continue
            other = from_partner(filtered, "half", 0)
            head = (filtered[:, :1] - other[:, :1]) ** 2
            tail = (filtered[:, -1:] - other[:, -1:]) ** 2
            low = lax.ppermute(tail, ("particle", "slab"), forward)
            high_rows = lax.ppermute(head, ("particle", "slab"), backward)
            sums = blend(
                filtered, other, low, high_rows, sums, CHUNK_BANDS, start + CHUNK_BANDS >= bands
            )
    return sums[None]


def solution(mesh):
    placed = (
        P("half", "particle", "slab", None),
        P("half", "particle", "slab"),
        P("half", "particle"),
        P("half", None),
        P(),
    )
    return jax.shard_map(
        on_device,
        mesh=mesh,
        in_specs=placed,
        out_specs=P("half", None, ("particle", "slab"), None),
        check_vma=False,
    )
```
